256 devices in a mesh: row: 16 (over x, z_hi), col: 16 (over y, z_lo, core).
Axes of the slice: x: 4, y: 4, z: 8 (z_hi: 4, z_lo: 2; z = z_hi * 2 + z_lo), core: 2. Of those that a mesh axis runs over, the one named last changes fastest.
Arguments:
- left_panels: bfloat16 [8192, 16384], P('row', 'col'), may hold values from -0.09375 to 0.09375
- right_panels: bfloat16 [16384, 32768], P('row', 'col'), may hold values from -6 to 6
- left_pattern: int32 [64, 128], P('row', 'col'), may hold values from 0 to 1, as said below
- right_pattern: int32 [128, 256], P('row', 'col'), may hold values from 0 to 1, as said below
Outputs:
- square_part: bfloat16 [8192, 32768], P('row', 'col')
The draws below stay inside these ranges and needn't reach their ends.
Inputs may be any that keep to these rules, and one draw needn't show every extreme that they name: `left_pattern`: entries are 0 or 1. In every block of 4 x 8 tiles held by one device at most 24 tiles are 1, and exactly 24 in at least one block. `right_pattern`: entries are 0 or 1. In every block of 8 x 16 tiles held by one device at most 96 tiles are 1, and exactly 96 in at least one block.
All inputs are finite; a program needn't handle non-finite values.
Results may differ from the reference program's by a relative error of at most 0.001.
Values may be sent and summed in bfloat16 or wider, within the bound.
A program may use at most 128 MiB of HBM per device.

```python
import jax
import jax.numpy as jnp
from jax import lax

TILE = 128
RT = 4
KT = 8
CT = 16
STEPS = 4
CAP = 24
CAPB = 96
MT = 64
KA = 128
KB = 128
NT = 256
N_ROW = 16
N_COL = 16


def tile_pattern(key, all_rows, all_cols, block_rows, block_cols, most):
    grid_rows = all_rows // block_rows
    grid_cols = all_cols // block_cols
    key_total, key_pick, key_weight, key_jitter = jax.random.split(key, 4)
    totals = jax.random.randint(key_total, (grid_rows, grid_cols), most // 2, most + 1)
    picked = jax.random.randint(key_pick, (), 0, grid_rows * grid_cols)
    block_ids = jnp.arange(grid_rows * grid_cols, dtype=jnp.int32).reshape(grid_rows, grid_cols)
    totals = jnp.where(block_ids == picked, most, totals)
    row_weight = jax.random.randint(key_weight, (all_rows, 1), 0, 4)
    row_weight = row_weight * row_weight
    jitter_bits = jax.random.randint(key_jitter, (all_rows, all_cols), 0, 1024)
    row_place = jnp.arange(all_rows, dtype=jnp.int32) % block_rows
    col_place = jnp.arange(all_cols, dtype=jnp.int32) % block_cols
    within = row_place[:, None] * block_cols + col_place[None, :]
    tile_score = (row_weight * 1024 + jitter_bits) * (block_rows * block_cols) + within
    grouped = tile_score.reshape(grid_rows, block_rows, grid_cols, block_cols)
    grouped = grouped.transpose(0, 2, 1, 3).reshape(grid_rows, grid_cols, block_rows * block_cols)
    sorted_slots = jnp.argsort(-grouped, axis=-1)
    slot_rank = jnp.argsort(sorted_slots, axis=-1)
    chosen = (slot_rank < totals[:, :, None]).astype(jnp.int32)
    chosen = chosen.reshape(grid_rows, grid_cols, block_rows, block_cols).transpose(0, 2, 1, 3)
    return chosen.reshape(all_rows, all_cols)


def draw_left_pattern(key, part):
    key = jax.random.fold_in(key, 11)
    return tile_pattern(key, MT, KA, RT, KT, CAP)


def draw_right_pattern(key, part):
    key = jax.random.fold_in(key, 23)
    return tile_pattern(key, KB, NT, KT, CT, CAPB)


def steps_of(stream_key, dims, shards, smallest, top_value):
    def one(dim, parts):
        steps = jax.random.uniform(jax.random.fold_in(jax.random.fold_in(stream_key, 6), dim), (parts,), jnp.float32, smallest / len(shards), top_value / len(shards))
        return jnp.repeat(jnp.exp(steps), dims[dim] // parts).reshape((-1,) + (1,) * (len(dims) - dim - 1))

    loudness = one(*shards[0])
    for cut in shards[1:]:
        loudness = loudness * one(*cut)
    return loudness


def gaussian(rng, extent, scale, limit, cuts=(), kind=jnp.bfloat16):
    values = scale * jax.random.normal(rng, extent, jnp.float32)
    if cuts:
        values = values * steps_of(rng, extent, cuts, -0.22, 0.18)
    return jnp.clip(values, -limit, limit).astype(kind)


def setup_inputs(seed: int = 0) -> dict:
    key_of = jax.random.split(jax.random.key(seed), 5)
    left_panels = gaussian(key_of[0], (MT * TILE, KA * TILE), (STEPS * KT * TILE) ** -0.5, 0.09375, ((0, 16), (1, 16)))
    right_panels = gaussian(key_of[1], (KB * TILE, NT * TILE), 1.0, 6.0, ((0, 16), (1, 16)))
    left_pattern = draw_left_pattern(jax.random.fold_in(key_of[4], 71), 0)
    right_pattern = draw_right_pattern(jax.random.fold_in(key_of[4], 71), 0)
    return dict(left_panels=left_panels, right_panels=right_panels, left_pattern=left_pattern, right_pattern=right_pattern)


def mask_tiles(matrix, occupancy):
    tile_rows, tile_cols = occupancy.shape
    view = matrix.reshape(tile_rows, TILE, tile_cols, TILE)
    view = view * occupancy.astype(matrix.dtype)[:, None, :, None]
    return view.reshape(matrix.shape)


def reference(left_panels, right_panels, left_pattern, right_pattern):
    masked_left = mask_tiles(left_panels, left_pattern)
    masked_right = mask_tiles(right_panels, right_pattern)
    left_grid = masked_left.reshape(N_ROW, RT * TILE, N_COL, KT * TILE)
    right_grid = masked_right.reshape(N_ROW, KT * TILE, N_COL, CT * TILE)

    def one_band(row_index):
        band = left_grid[row_index].astype(jnp.float32)
        running = jnp.zeros((RT * TILE, N_COL, CT * TILE), jnp.float32)
        for offset in range(STEPS):
            moved = jnp.roll(band, -offset, axis=1)
            source = ((row_index + offset) % N_ROW).astype(jnp.int32)
            other = lax.dynamic_index_in_dim(right_grid, source, 0, keepdims=False).astype(jnp.float32)
            running = running + jnp.einsum("ajk,kjb->ajb", moved, other, precision=lax.Precision.HIGHEST)
        return running.astype(jnp.bfloat16)

    result = lax.map(one_band, jnp.arange(N_ROW, dtype=jnp.int32))
    return result.reshape(MT * TILE, NT * TILE)
```

```python
import functools

import jax
import jax.numpy as jnp
from jax import lax
from jax.experimental import pallas as pl
from jax.experimental.pallas import tpu as pltpu
from jax.sharding import PartitionSpec as P

TILE = 128
RT, KT, CT = 4, 8, 16
CAP, CAPB = 24, 96
CHUNKS = 4
PER = CAPB // CHUNKS
WIDE = 256
PIECES = CT * TILE // WIDE
GROUPS = 8
SPAN = RT * TILE // GROUPS
TOP = 32767.0
MESH = pl.DeviceIdType.MESH
SLOT_B, SLOT_A, PICK_B, PICK_A = 0, 1, 2, 3
LOCAL, WITH_OWN, WITH_NEXT, NEXT, FAR = range(5)


def tables_kernel(left_ref, right_ref, table_ref):
    def clear(i, carry):
        table_ref[PICK_B, i] = 0
        table_ref[PICK_A, i] = 0
        table_ref[SLOT_A, i] = CAP
        return carry

    lax.fori_loop(0, TILE, clear, 0)

    def walk_right(t, taken):
        there = right_ref[t % KT, t // KT]
        table_ref[PICK_B, jnp.minimum(taken, TILE - 1)] = t
        table_ref[SLOT_B, t] = jnp.where(there > 0, taken, CAPB)
        return taken + jnp.where(there > 0, 1, 0)

    lax.fori_loop(0, KT * CT, walk_right, 0)

    def walk_left(t, taken):
        there = left_ref[t % RT, t // RT]
        table_ref[PICK_A, jnp.minimum(taken, TILE - 1)] = t
        table_ref[SLOT_A, t] = jnp.where(there > 0, taken, CAP)
        return taken + jnp.where(there > 0, 1, 0)

    lax.fori_loop(0, RT * KT, walk_left, 0)


def main_kernel(
    a_ref, b_ref, table_ref, table_hbm, out_ref,
    a_in, b_in, a_pack, b_pack, a_got, b_got, b_stage, table_got, table_at,
    a_full, b_full, total, part, code_out, scale_out, code_in, scale_in, result,
    local_sem, table_send, table_recv, a_send, a_recv, b_send, b_recv, p_send, p_recv, out_sem,
):
    n_row, n_col = lax.axis_size("row"), lax.axis_size("col")
    row, col = lax.axis_index("row"), lax.axis_index("col")
    odd = lax.rem(row + col, 2)

    def at(i, j):
        return (lax.rem(row + i + n_row, n_row), lax.rem(col + j + n_col, n_col))

    targets = (at(0, 2 * odd - 3), at(1 + 2 * odd, -1 - 2 * odd), at(3 - 2 * odd, -2), at(1 - 2 * odd, 0), at(-4, 0))
    sources = (at(0, 1 + 2 * odd), at(-1 - 2 * odd, 1 + 2 * odd), at(-1 - 2 * odd, 2), at(1 - 2 * odd, 0), at(4, 0))
    p_target, p_source = at(-1 - 2 * odd, 0), at(3 - 2 * odd, 0)

    barrier = pltpu.get_barrier_semaphore()
    for source in (*sources[:4], p_source):
        pl.semaphore_signal(barrier, inc=1, device_id=source, device_id_type=MESH)

    @pl.when(odd == 1)
    def _():
        pl.semaphore_signal(barrier, inc=1, device_id=sources[FAR], device_id_type=MESH)

    def load_a(k):
        return pltpu.make_async_copy(
            a_ref.at[:, :, pl.ds(k * TILE, TILE)], a_in.at[pl.ds(k * RT, RT)], local_sem.at[k])

    def load_b(c):
        return pltpu.make_async_copy(
            b_ref.at[:, :, pl.ds(c * TILE, TILE)], b_in.at[pl.ds(c * KT, KT)], local_sem.at[KT + c])

    for k in range(KT):
        load_a(k).start()
    for c in range(CT):
        load_b(c).start()

    blank = jnp.zeros((TILE, TILE), jnp.bfloat16)
    a_pack[CAP] = blank
    b_pack[CAPB] = blank
    for i in range(3):
        a_got[i, CAP] = blank
    b_got[1, CAPB] = blank
    b_stage[CAPB] = blank

    def pack_a(n, carry):
        a_pack[n] = a_in[table_ref[PICK_A, n]]
        return carry

    def pack_b(n, carry):
        b_pack[n] = b_in[table_ref[PICK_B, n]]
        return carry

    def stage_b(n, carry):
        b_stage[n] = b_got[0, n]
        return carry

    def send_table(i, source):
        return pltpu.make_async_remote_copy(
            source, table_got.at[i], table_send.at[i], table_recv.at[i], device_id=targets[i], device_id_type=MESH)

    def send_a(i):
        return pltpu.make_async_remote_copy(
            a_pack.at[pl.ds(0, CAP)], a_got.at[i, pl.ds(0, CAP)], a_send.at[i], a_recv.at[i],
            device_id=targets[i], device_id_type=MESH)

    def send_b(i, q, source):
        where = pl.ds(q * PER, PER)
        return pltpu.make_async_remote_copy(
            source.at[where], b_got.at[i, where], b_send.at[i, q], b_recv.at[i, q],
            device_id=targets[NEXT + i], device_id_type=MESH)

    def send_code(c):
        return pltpu.make_async_remote_copy(
            code_out.at[c], code_in.at[c], p_send.at[0, c], p_recv.at[0, c], device_id=p_target, device_id_type=MESH)

    def send_scale(c):
        return pltpu.make_async_remote_copy(
            scale_out.at[c], scale_in.at[c], p_send.at[1, c], p_recv.at[1, c], device_id=p_target, device_id_type=MESH)

    for k in range(KT):
        load_a(k).wait()
    lax.fori_loop(0, CAP, pack_a, 0)
    pl.semaphore_wait(barrier, 5 + odd)
    for i in range(4):
        send_table(i, table_hbm).start()
    for i in (WITH_OWN, WITH_NEXT, LOCAL):
        send_a(i).start()
    for c in range(CT):
        load_b(c).wait()
    for q in range(CHUNKS):
        lax.fori_loop(q * PER, (q + 1) * PER, pack_b, 0)
        send_b(0, q, b_pack).start()

    def unpack_a(i, tile_of):
        for k in range(KT):
            for r in range(RT):
                a_full[i, r * TILE : (r + 1) * TILE, k * TILE : (k + 1) * TILE] = tile_of(k * RT + r)

    def unpack_b(i, tile_of, first, last):
        def one(c, carry):
            for half in range(WIDE // TILE):
                for k in range(KT):
                    tile = tile_of((c * (WIDE // TILE) + half) * KT + k)
                    b_full[i, c, k * TILE : (k + 1) * TILE, half * TILE : (half + 1) * TILE] = tile
            return carry

        lax.fori_loop(first, last, one, 0)

    def product(i, j, c):
        return jnp.dot(a_full[i], b_full[j, c], preferred_element_type=jnp.float32)

    unpack_a(3, lambda t: a_pack[table_ref[SLOT_A, t]])
    unpack_b(0, lambda t: b_pack[table_ref[SLOT_B, t]], 0, PIECES)

    def first_term(c, carry):
        total[c] = product(3, 0, c)
        return carry

    lax.fori_loop(0, PIECES, first_term, 0)

    def fetch_table(i):
        send_table(i, table_hbm).wait_recv()
        fetch = pltpu.make_async_copy(table_got.at[i], table_at.at[i], local_sem.at[KT + CT])
        fetch.start()
        fetch.wait()

    for i in (WITH_OWN, WITH_NEXT, LOCAL):
        fetch_table(i)
        send_a(i).wait_recv()
    for i in (WITH_OWN, WITH_NEXT, LOCAL):
        unpack_a(i, lambda t: a_got[i, table_at[i, SLOT_A, t]])

    def part_own(c, carry):
        part[c] = product(WITH_OWN, 0, c)
        return carry

    lax.fori_loop(0, PIECES, part_own, 0)
    fetch_table(NEXT)

    @pl.when(odd == 1)
    def _():
        send_table(FAR, table_got.at[NEXT]).start()

    def send_part(c, carry):
        part[c] += product(WITH_NEXT, 1, c)
        for g in range(GROUPS):
            rows = slice(g * SPAN, (g + 1) * SPAN)
            values = part[c, rows, :]
            most = jnp.maximum(jnp.max(jnp.abs(values), axis=0, keepdims=True), 1e-33)
            code_out[c, rows, :] = jnp.round(values * (TOP / most)).astype(jnp.int32).astype(jnp.int16)
            scale_out[c, g : g + 1, :] = most * (1.0 / TOP)
        send_scale(c).start()
        send_code(c).start()
        return carry

    done = 0
    for q in range(CHUNKS):
        send_b(0, q, b_pack).wait_recv()

        @pl.when(odd == 1)
        def _():
            send_b(1, q, b_got.at[0]).start()

        lax.fori_loop(q * PER, (q + 1) * PER, stage_b, 0)
        ready = PIECES if q == CHUNKS - 1 else (q + 1) * PER // KT * TILE // WIDE
        if q >= CHUNKS - 2:
            unpack_b(1, lambda t: b_stage[table_at[NEXT, SLOT_B, t]], done, ready)
            lax.fori_loop(done, ready, send_part, 0)
            done = ready

    @pl.when(odd == 1)
    def _():
        fetch_table(FAR)
        for q in range(CHUNKS):
            send_b(1, q, b_got.at[0]).wait_recv()
        unpack_b(1, lambda t: b_got[1, table_at[FAR, SLOT_B, t]], 0, PIECES)

    def second_term(c, carry):
        total[c] += product(LOCAL, 1, c)
        return carry

    lax.fori_loop(0, PIECES, second_term, 0)

    def store(c):
        return pltpu.make_async_copy(result.at[c], out_ref.at[:, pl.ds(c * WIDE, WIDE)], out_sem.at[c])

    for c in range(PIECES):
        send_scale(c).wait_recv()
        send_code(c).wait_recv()
        for g in range(GROUPS):
            rows = slice(g * SPAN, (g + 1) * SPAN)
            other = code_in[c, rows, :].astype(jnp.int32).astype(jnp.float32) * scale_in[c, g : g + 1, :]
            result[c, rows, :] = (total[c, rows, :] + other).astype(jnp.bfloat16)
        store(c).start()

    for i in range(4):
        send_table(i, table_hbm).wait_send()
    for i in range(3):
        send_a(i).wait_send()
    for q in range(CHUNKS):
        send_b(0, q, b_pack).wait_send()

    @pl.when(odd == 1)
    def _():
        send_table(FAR, table_got.at[NEXT]).wait_send()
        for q in range(CHUNKS):
            send_b(1, q, b_got.at[0]).wait_send()

    for c in range(PIECES):
        send_scale(c).wait_send()
        send_code(c).wait_send()
        store(c).wait()


def per_device(left_panels, right_panels, left_pattern, right_pattern):
    smem = pl.BlockSpec(memory_space=pltpu.SMEM)
    anywhere = pl.BlockSpec(memory_space=pl.ANY)
    table = pl.pallas_call(
        tables_kernel,
        out_shape=jax.ShapeDtypeStruct((4, TILE), jnp.int32),
        in_specs=[smem, smem],
        out_specs=smem,
        name="tile_tables",
    )(left_pattern, right_pattern)
    rows, cols, inner = RT * TILE, CT * TILE, KT * TILE
    bf16, f32, dma = jnp.bfloat16, jnp.float32, pltpu.SemaphoreType.DMA
    return pl.pallas_call(
        main_kernel,
        out_shape=jax.ShapeDtypeStruct((rows, cols), bf16),
        in_specs=[anywhere, anywhere, smem, anywhere],
        out_specs=anywhere,
        scratch_shapes=[
            pltpu.VMEM((RT * KT, TILE, TILE), bf16),
            pltpu.VMEM((KT * CT, TILE, TILE), bf16),
            pltpu.VMEM((CAP + 1, TILE, TILE), bf16),
            pltpu.VMEM((CAPB + 1, TILE, TILE), bf16),
            pltpu.VMEM((3, CAP + 1, TILE, TILE), bf16),
            pltpu.VMEM((2, CAPB + 1, TILE, TILE), bf16),
            pltpu.VMEM((CAPB + 1, TILE, TILE), bf16),
            pltpu.VMEM((5, 4, TILE), jnp.int32),
            pltpu.SMEM((5, 4, TILE), jnp.int32),
            pltpu.VMEM((4, rows, inner), bf16),
            pltpu.VMEM((2, PIECES, inner, WIDE), bf16),
            pltpu.VMEM((PIECES, rows, WIDE), f32),
            pltpu.VMEM((PIECES, rows, WIDE), f32),
            pltpu.VMEM((PIECES, rows, WIDE), jnp.int16),
            pltpu.VMEM((PIECES, GROUPS, WIDE), f32),
            pltpu.VMEM((PIECES, rows, WIDE), jnp.int16),
            pltpu.VMEM((PIECES, GROUPS, WIDE), f32),
            pltpu.VMEM((PIECES, rows, WIDE), bf16),
            dma((KT + CT + 1,)),
            dma((5,)),
            dma((5,)),
            dma((3,)),
            dma((3,)),
            dma((2, CHUNKS)),
            dma((2, CHUNKS)),
            dma((2, PIECES)),
            dma((2, PIECES)),
            dma((PIECES,)),
        ],
        compiler_params=pltpu.CompilerParams(
            collective_id=0, has_side_effects=True, vmem_limit_bytes=60 * 2**20
        ),
        cost_estimate=pl.CostEstimate(flops=8 * rows * inner * cols, bytes_accessed=2**23, transcendentals=0),
        name="exchange_and_multiply",
    )(left_panels.reshape(RT, TILE, inner), right_panels.reshape(KT, TILE, cols), table, table)


def solution(mesh):
    placed = (P("row", "col"), P("row", "col"), P("row", "col"), P("row", "col"))
    return jax.shard_map(
        per_device, mesh=mesh, in_specs=placed, out_specs=P("row", "col"), check_vma=False
    )
```

```python
import functools

import jax
import jax.numpy as jnp
from jax import lax
from jax.experimental import pallas as pl
from jax.experimental.pallas import tpu as pltpu
from jax.sharding import PartitionSpec as P

TILE = 128
RT, KT, CT = 4, 8, 16
CAP, CAPB = 24, 96
CHUNKS = 8
PER = CAPB // CHUNKS
WIDE = 256
PIECES = CT * TILE // WIDE
GROUPS = 8
SPAN = RT * TILE // GROUPS
TOP = 32767.0
MESH = pl.DeviceIdType.MESH
WITH_OWN, WITH_NEXT, LOCAL, NEXT, FAR = range(5)
TAKERS = (
    (WITH_OWN, 1, -1, 0), (WITH_OWN, 3, -3, 1),
    (WITH_NEXT, 1, -2, 0), (WITH_NEXT, 3, -2, 1),
    (LOCAL, 0, -1, 0), (LOCAL, 0, -3, 1),
)


def main_kernel(
    a_ref, b_ref, left_ref, right_ref, out_ref,
    a_slot, b_slot, a_after, b_after, a_table, b_table,
    a_in, b_in, a_pack, b_pack, a_got, a_near, b_got, b_stage, table_got, table_at,
    a_full, b_full, total, part, code_out, scale_out, code_in, scale_in, result,
    local_sem, table_send, table_recv, a_send, a_recv, b_send, b_recv, p_send, p_recv, out_sem,
):
    n_row, n_col = lax.axis_size("row"), lax.axis_size("col")
    row, col = lax.axis_index("row"), lax.axis_index("col")

    def at(i, j):
        return (lax.rem(row + i + n_row, n_row), lax.rem(col + j + n_col, n_col))

    def parity(i, j):
        return lax.rem(i + j, 2)

    odd = parity(row, col)
    takes = [jnp.where(parity(*at(i, j)) == want, 1, 0) for _, i, j, want in TAKERS]
    b_target, b_source = at(1 - 2 * odd, 0), at(1 - 2 * odd, 0)
    p_target, p_source = at(-1 - 2 * odd, 0), at(3 - 2 * odd, 0)
    far_target, far_source = at(-4, 0), at(4, 0)
    a_sources = (at(-1 - 2 * odd, 1 + 2 * odd), at(-1 - 2 * odd, 2), at(0, 1 + 2 * odd))

    barrier = pltpu.get_barrier_semaphore()
    for source in (*a_sources, b_source, p_source):
        pl.semaphore_signal(barrier, inc=1, device_id=source, device_id_type=MESH)

    @pl.when(odd == 1)
    def _():
        pl.semaphore_signal(barrier, inc=1, device_id=far_source, device_id_type=MESH)

    def load_a(k):
        return pltpu.make_async_copy(
            a_ref.at[:, :, pl.ds(k * TILE, TILE)], a_in.at[pl.ds(k * RT, RT)], local_sem.at[k])

    def load_b(c):
        return pltpu.make_async_copy(
            b_ref.at[:, :, pl.ds(c * TILE, TILE)], b_in.at[pl.ds(c * KT, KT)], local_sem.at[KT + c])

    for k in range(KT):
        load_a(k).start()
    for c in range(CT):
        load_b(c).start()

    blank = jnp.zeros((TILE, TILE), jnp.bfloat16)
    a_pack[CAP] = blank
    b_pack[CAPB] = blank
    for i in range(2):
        a_got[i, CAP] = blank
    a_near[CAP] = blank
    b_got[1, CAPB] = blank
    b_stage[CAPB] = blank

    def number(there, count, slot, after, blank_slot):
        def walk(t, taken):
            slot[0, t] = jnp.where(there(t) > 0, taken, blank_slot)
            return taken + jnp.where(there(t) > 0, 1, 0)

        lax.fori_loop(0, count, walk, 0)

        def back(n, found):
            t = count - 1 - n
            found = jnp.where(there(t) > 0, t, found)
            after[0, t] = found
            return found

        after[0, count] = count - 1
        lax.fori_loop(0, count, back, count - 1)

    def pack_a(n, start):
        t = a_after[0, start]
        a_pack[n] = a_in[t]
        return t + 1

    def pack_b(n, start):
        t = b_after[0, start]
        b_pack[n] = b_in[t]
        return t + 1

    def stage_b(n, carry):
        b_stage[n] = b_got[0, n]
        return carry

    def send_table(n, i, source, target):
        return pltpu.make_async_remote_copy(
            source, table_got.at[i], table_send.at[n], table_recv.at[i], device_id=target, device_id_type=MESH)

    def send_a(n):
        use, i, j, _ = TAKERS[n]
        place = a_near if use == LOCAL else a_got.at[use]
        return pltpu.make_async_remote_copy(
            a_pack.at[pl.ds(0, CAP)], place.at[pl.ds(0, CAP)], a_send.at[n], a_recv.at[use],
            device_id=at(i, j), device_id_type=MESH)

    def each_taker(uses, act):
        for n, (use, i, j, _) in enumerate(TAKERS):
            if use in uses:

                @pl.when(takes[n] == 1)
                def _():
                    act(send_table(n, use, a_table, at(i, j)))
                    act(send_a(n))

    def send_b(q):
        where = pl.ds(q * PER, PER)
        return pltpu.make_async_remote_copy(
            b_pack.at[where], b_got.at[0, where], b_send.at[0, q], b_recv.at[0, q],
            device_id=b_target, device_id_type=MESH)

    def send_far(q):
        where = pl.ds(q * PER, PER)
        return pltpu.make_async_remote_copy(
            b_got.at[0, where], b_got.at[1, where], b_send.at[1, q], b_recv.at[1, q],
            device_id=far_target, device_id_type=MESH)

    next_table = send_table(len(TAKERS), NEXT, b_table, b_target)
    far_table = send_table(len(TAKERS) + 1, FAR, table_got.at[NEXT], far_target)

    def send_code(c):
        return pltpu.make_async_remote_copy(
            code_out.at[c], code_in.at[c], p_send.at[0, c], p_recv.at[0, c], device_id=p_target, device_id_type=MESH)

    def send_scale(c):
        return pltpu.make_async_remote_copy(
            scale_out.at[c], scale_in.at[c], p_send.at[1, c], p_recv.at[1, c], device_id=p_target, device_id_type=MESH)

    def publish(slot, table):
        copy = pltpu.make_async_copy(slot, table, local_sem.at[KT + CT])
        copy.start()
        copy.wait()

    number(lambda t: left_ref[t % RT, t // RT], RT * KT, a_slot, a_after, CAP)
    publish(a_slot, a_table)
    for k in range(KT):
        load_a(k).wait()
    lax.fori_loop(0, CAP, pack_a, 0)
    pl.semaphore_wait(barrier, 2 + odd + sum(takes))
    each_taker((WITH_OWN, WITH_NEXT), lambda copy: copy.start())
    number(lambda t: right_ref[t % KT, t // KT], KT * CT, b_slot, b_after, CAPB)
    publish(b_slot, b_table)
    next_table.start()
    for c in range(CT):
        load_b(c).wait()
    lax.fori_loop(0, CAPB, pack_b, 0)
    send_b(0).start()
    send_b(1).start()

    def unpack_a(i, tile_of):
        for k in range(KT):
            for r in range(RT):
                a_full[i, r * TILE : (r + 1) * TILE, k * TILE : (k + 1) * TILE] = tile_of(k * RT + r)

    def unpack_b(i, tile_of, first, last):
        def one(c, carry):
            for half in range(WIDE // TILE):
                for k in range(KT):
                    tile = tile_of((c * (WIDE // TILE) + half) * KT + k)
                    b_full[i, c, k * TILE : (k + 1) * TILE, half * TILE : (half + 1) * TILE] = tile
            return carry

        lax.fori_loop(first, last, one, 0)

    def product(i, j, c):
        return jnp.dot(a_full[i], b_full[j, c], preferred_element_type=jnp.float32)

    unpack_a(3, lambda t: a_pack[a_slot[0, t]])
    unpack_b(0, lambda t: b_pack[b_slot[0, t]], 0, PIECES)

    def first_term(c, carry):
        total[c] = product(3, 0, c)
        return carry

    lax.fori_loop(0, PIECES, first_term, 0)

    def fetch_table(i):
        send_table(0, i, a_table, b_target).wait_recv()
        fetch = pltpu.make_async_copy(table_got.at[i], table_at.at[i], local_sem.at[KT + CT])
        fetch.start()
        fetch.wait()

    fetch_table(NEXT)

    @pl.when(odd == 1)
    def _():
        far_table.start()

    def part_own(c, carry):
        part[c] = product(WITH_OWN, 0, c)
        return carry

    early = CHUNKS - PIECES // 2
    for q in range(CHUNKS):
        if q + 2 < CHUNKS:
            send_b(q).wait_send()
            send_b(q + 2).start()
        if q == early:
            for i in (WITH_OWN, WITH_NEXT):
                fetch_table(i)
                send_a(2 * i).wait_recv()
            for i in (WITH_OWN, WITH_NEXT):
                unpack_a(i, lambda t: a_got[i, table_at[i, 0, t]])
        if q >= early:
            lax.fori_loop(2 * (q - early), 2 * (q - early) + 2, part_own, 0)
        send_b(q).wait_recv()

        @pl.when(odd == 1)
        def _():
            send_far(q).start()

        lax.fori_loop(q * PER, (q + 1) * PER, stage_b, 0)

    for c in range(PIECES):
        unpack_b(1, lambda t: b_stage[table_at[NEXT, 0, t]], c, c + 1)
        part[c] += product(WITH_NEXT, 1, c)
        for g in range(GROUPS):
            rows = slice(g * SPAN, (g + 1) * SPAN)
            values = part[c, rows, :]
            most = jnp.maximum(jnp.max(jnp.abs(values), axis=0, keepdims=True), 1e-33)
            code_out[c, rows, :] = jnp.round(values * (TOP / most)).astype(jnp.int32).astype(jnp.int16)
            scale_out[c, g : g + 1, :] = most * (1.0 / TOP)
        if c >= 3:
            send_code(c - 3).wait_send()
        send_scale(c).start()
        send_code(c).start()
        if c == 1:
            each_taker((LOCAL,), lambda copy: copy.start())

    @pl.when(odd == 1)
    def _():
        fetch_table(FAR)
        for q in range(CHUNKS):
            send_far(q).wait_recv()
        unpack_b(1, lambda t: b_got[1, table_at[FAR, 0, t]], 0, PIECES)

    fetch_table(LOCAL)
    send_a(2 * LOCAL).wait_recv()
    unpack_a(LOCAL, lambda t: a_near[table_at[LOCAL, 0, t]])

    def second_term(c, carry):
        total[c] += product(LOCAL, 1, c)
        return carry

    lax.fori_loop(0, PIECES, second_term, 0)

    def store(c):
        return pltpu.make_async_copy(result.at[c], out_ref.at[:, pl.ds(c * WIDE, WIDE)], out_sem.at[c])

    for c in range(PIECES):
        send_scale(c).wait_recv()
        send_code(c).wait_recv()
        for g in range(GROUPS):
            rows = slice(g * SPAN, (g + 1) * SPAN)
            other = code_in[c, rows, :].astype(jnp.int32).astype(jnp.float32) * scale_in[c, g : g + 1, :]
            result[c, rows, :] = (total[c, rows, :] + other).astype(jnp.bfloat16)
        store(c).start()

    each_taker((WITH_OWN, WITH_NEXT, LOCAL), lambda copy: copy.wait_send())
    next_table.wait_send()
    for q in range(CHUNKS - 2, CHUNKS):
        send_b(q).wait_send()

    @pl.when(odd == 1)
    def _():
        far_table.wait_send()
        for q in range(CHUNKS):
            send_far(q).wait_send()

    for c in range(PIECES):
        send_scale(c).wait_send()
        if c >= PIECES - 3:
            send_code(c).wait_send()
        store(c).wait()


def per_device(left_panels, right_panels, left_pattern, right_pattern):
    smem = pl.BlockSpec(memory_space=pltpu.SMEM)
    anywhere = pl.BlockSpec(memory_space=pl.ANY)
    rows, cols, inner = RT * TILE, CT * TILE, KT * TILE
    bf16, f32, dma = jnp.bfloat16, jnp.float32, pltpu.SemaphoreType.DMA
    return pl.pallas_call(
        main_kernel,
        out_shape=jax.ShapeDtypeStruct((rows, cols), bf16),
        in_specs=[anywhere, anywhere, smem, smem],
        out_specs=anywhere,
        scratch_shapes=[
            pltpu.SMEM((1, TILE), jnp.int32),
            pltpu.SMEM((1, TILE), jnp.int32),
            pltpu.SMEM((1, 2 * TILE), jnp.int32),
            pltpu.SMEM((1, 2 * TILE), jnp.int32),
            pltpu.VMEM((1, TILE), jnp.int32),
            pltpu.VMEM((1, TILE), jnp.int32),
            pltpu.VMEM((RT * KT, TILE, TILE), bf16),
            pltpu.VMEM((KT * CT, TILE, TILE), bf16),
            pltpu.VMEM((CAP + 1, TILE, TILE), bf16),
            pltpu.VMEM((CAPB + 1, TILE, TILE), bf16),
            pltpu.VMEM((2, CAP + 1, TILE, TILE), bf16),
            pltpu.VMEM((CAP + 1, TILE, TILE), bf16),
            pltpu.VMEM((2, CAPB + 1, TILE, TILE), bf16),
            pltpu.VMEM((CAPB + 1, TILE, TILE), bf16),
            pltpu.VMEM((5, 1, TILE), jnp.int32),
            pltpu.SMEM((5, 1, TILE), jnp.int32),
            pltpu.VMEM((4, rows, inner), bf16),
            pltpu.VMEM((2, PIECES, inner, WIDE), bf16),
            pltpu.VMEM((PIECES, rows, WIDE), f32),
            pltpu.VMEM((PIECES, rows, WIDE), f32),
            pltpu.VMEM((PIECES, rows, WIDE), jnp.int16),
            pltpu.VMEM((PIECES, GROUPS, WIDE), f32),
            pltpu.VMEM((PIECES, rows, WIDE), jnp.int16),
            pltpu.VMEM((PIECES, GROUPS, WIDE), f32),
            pltpu.VMEM((PIECES, rows, WIDE), bf16),
            dma((KT + CT + 1,)),
            dma((len(TAKERS) + 2,)),
            dma((5,)),
            dma((len(TAKERS),)),
            dma((3,)),
            dma((2, CHUNKS)),
            dma((2, CHUNKS)),
            dma((2, PIECES)),
            dma((2, PIECES)),
            dma((PIECES,)),
        ],
        compiler_params=pltpu.CompilerParams(
            collective_id=0, has_side_effects=True, vmem_limit_bytes=60 * 2**20
        ),
        cost_estimate=pl.CostEstimate(flops=8 * rows * inner * cols, bytes_accessed=2**23, transcendentals=0),
        name="exchange_and_multiply",
    )(left_panels.reshape(RT, TILE, inner), right_panels.reshape(KT, TILE, cols), left_pattern, right_pattern)


def solution(mesh):
    placed = (P("row", "col"), P("row", "col"), P("row", "col"), P("row", "col"))
    return jax.shard_map(
        per_device, mesh=mesh, in_specs=placed, out_specs=P("row", "col"), check_vma=False
    )
```

```python
import functools

import jax
import jax.numpy as jnp
from jax import lax
from jax.experimental import pallas as pl
from jax.experimental.pallas import tpu as pltpu
from jax.sharding import PartitionSpec as P

TILE = 128
RT, KT, CT = 4, 8, 16
CAP, CAPB = 24, 96
CHUNKS = 8
PER = CAPB // CHUNKS
WIDE = 256
PIECES = CT * TILE // WIDE
GROUPS = 8
SPAN = RT * TILE // GROUPS
TOP = 32767.0
MESH = pl.DeviceIdType.MESH
WITH_OWN, WITH_NEXT, LOCAL, NEXT, FAR = range(5)
TAKERS = (
    (WITH_OWN, 1, -1, 0), (WITH_OWN, 3, -3, 1),
    (WITH_NEXT, 1, -2, 0), (WITH_NEXT, 3, -2, 1),
    (LOCAL, 0, -1, 0), (LOCAL, 0, -3, 1),
)


def main_kernel(
    a_ref, b_ref, left_ref, right_ref, out_ref,
    a_slot, b_slot, a_after, b_after, a_table, b_table,
    a_in, b_in, a_pack, b_pack, a_got, a_near, b_got, b_stage, table_got, table_at,
    a_full, b_full, total, part, code_out, scale_out, code_in, scale_in, result,
    local_sem, table_send, table_recv, a_send, a_recv, b_send, b_recv, p_send, p_recv, out_sem,
):
    n_row, n_col = lax.axis_size("row"), lax.axis_size("col")
    row, col = lax.axis_index("row"), lax.axis_index("col")

    def at(i, j):
        return (lax.rem(row + i + n_row, n_row), lax.rem(col + j + n_col, n_col))

    def parity(i, j):
        return lax.rem(i + j, 2)

    odd = parity(row, col)
    takes = [jnp.where(parity(*at(i, j)) == want, 1, 0) for _, i, j, want in TAKERS]
    b_target, b_source = at(1 - 2 * odd, 0), at(1 - 2 * odd, 0)
    p_target, p_source = at(-1 - 2 * odd, 0), at(3 - 2 * odd, 0)
    far_target, far_source = at(-4, 0), at(4, 0)
    a_sources = (at(-1 - 2 * odd, 1 + 2 * odd), at(-1 - 2 * odd, 2), at(0, 1 + 2 * odd))

    barrier = pltpu.get_barrier_semaphore()
    for source in (*a_sources, b_source, p_source):
        pl.semaphore_signal(barrier, inc=1, device_id=source, device_id_type=MESH)

    @pl.when(odd == 1)
    def _():
        pl.semaphore_signal(barrier, inc=1, device_id=far_source, device_id_type=MESH)

    def load_a(k):
        return pltpu.make_async_copy(
            a_ref.at[:, :, pl.ds(k * TILE, TILE)], a_in.at[pl.ds(k * RT, RT)], local_sem.at[k])

    def load_b(c):
        return pltpu.make_async_copy(
            b_ref.at[:, :, pl.ds(c * TILE, TILE)], b_in.at[pl.ds(c * KT, KT)], local_sem.at[KT + c])

    for k in range(KT):
        load_a(k).start()
    for c in range(CT):
        load_b(c).start()

    blank = jnp.zeros((TILE, TILE), jnp.bfloat16)
    a_pack[CAP] = blank
    b_pack[CAPB] = blank
    for i in range(2):
        a_got[i, CAP] = blank
    a_near[CAP] = blank
    b_got[1, CAPB] = blank
    b_stage[CAPB] = blank

    def number(there, count, slot, after, blank_slot):
        def walk(t, taken):
            slot[0, t] = jnp.where(there(t) > 0, taken, blank_slot)
            return taken + jnp.where(there(t) > 0, 1, 0)

        lax.fori_loop(0, count, walk, 0)

        def back(n, found):
            t = count - 1 - n
            found = jnp.where(there(t) > 0, t, found)
            after[0, t] = found
            return found

        after[0, count] = count - 1
        lax.fori_loop(0, count, back, count - 1)

    def pack_a(n, start):
        t = a_after[0, start]
        a_pack[n] = a_in[t]
        return t + 1

    def pack_b(n, start):
        t = b_after[0, start]
        b_pack[n] = b_in[t]
        return t + 1

    def stage_b(n, carry):
        b_stage[n] = b_got[0, n]
        return carry

    def send_table(n, i, source, target):
        return pltpu.make_async_remote_copy(
            source, table_got.at[i], table_send.at[n], table_recv.at[i], device_id=target, device_id_type=MESH)

    def send_a(n):
        use, i, j, _ = TAKERS[n]
        place = a_near if use == LOCAL else a_got.at[use]
        return pltpu.make_async_remote_copy(
            a_pack.at[pl.ds(0, CAP)], place.at[pl.ds(0, CAP)], a_send.at[n], a_recv.at[use],
            device_id=at(i, j), device_id_type=MESH)

    def each_taker(uses, act):
        for n, (use, i, j, _) in enumerate(TAKERS):
            if use in uses:

                @pl.when(takes[n] == 1)
                def _():
                    act(send_table(n, use, a_table, at(i, j)))
                    act(send_a(n))

    def send_b(q):
        where = pl.ds(q * PER, PER)
        return pltpu.make_async_remote_copy(
            b_pack.at[where], b_got.at[0, where], b_send.at[0, q], b_recv.at[0, q],
            device_id=b_target, device_id_type=MESH)

    def send_far(q):
        where = pl.ds(q * PER, PER)
        return pltpu.make_async_remote_copy(
            b_got.at[0, where], b_got.at[1, where], b_send.at[1, q], b_recv.at[1, q],
            device_id=far_target, device_id_type=MESH)

    next_table = send_table(len(TAKERS), NEXT, b_table, b_target)
    far_table = send_table(len(TAKERS) + 1, FAR, table_got.at[NEXT], far_target)

    def send_code(c):
        return pltpu.make_async_remote_copy(
            code_out.at[c], code_in.at[c], p_send.at[0, c], p_recv.at[0, c], device_id=p_target, device_id_type=MESH)

    def send_scale(c):
        return pltpu.make_async_remote_copy(
            scale_out.at[c], scale_in.at[c], p_send.at[1, c], p_recv.at[1, c], device_id=p_target, device_id_type=MESH)

    def publish(slot, table):
        copy = pltpu.make_async_copy(slot, table, local_sem.at[KT + CT])
        copy.start()
        copy.wait()

    number(lambda t: left_ref[t % RT, t // RT], RT * KT, a_slot, a_after, CAP)
    publish(a_slot, a_table)
    for k in range(KT):
        load_a(k).wait()
    lax.fori_loop(0, CAP, pack_a, 0)
    pl.semaphore_wait(barrier, 2 + odd + sum(takes))
    each_taker((WITH_OWN, WITH_NEXT), lambda copy: copy.start())
    number(lambda t: right_ref[t % KT, t // KT], KT * CT, b_slot, b_after, CAPB)
    publish(b_slot, b_table)
    next_table.start()
    for c in range(CT):
        load_b(c).wait()
    lax.fori_loop(0, CAPB, pack_b, 0)
    send_b(0).start()

    def unpack_a(i, tile_of):
        for k in range(KT):
            for r in range(RT):
                a_full[i, r * TILE : (r + 1) * TILE, k * TILE : (k + 1) * TILE] = tile_of(k * RT + r)

    def unpack_b(i, tile_of, first, last):
        def one(c, carry):
            for half in range(WIDE // TILE):
                for k in range(KT):
                    tile = tile_of((c * (WIDE // TILE) + half) * KT + k)
                    b_full[i, c, k * TILE : (k + 1) * TILE, half * TILE : (half + 1) * TILE] = tile
            return carry

        lax.fori_loop(first, last, one, 0)

    def product(i, j, c):
        return jnp.dot(a_full[i], b_full[j, c], preferred_element_type=jnp.float32)

    unpack_a(3, lambda t: a_pack[a_slot[0, t]])
    unpack_b(0, lambda t: b_pack[b_slot[0, t]], 0, PIECES)

    def first_term(c, carry):
        total[c] = product(3, 0, c)
        return carry

    lax.fori_loop(0, PIECES, first_term, 0)

    def fetch_table(i):
        send_table(0, i, a_table, b_target).wait_recv()
        fetch = pltpu.make_async_copy(table_got.at[i], table_at.at[i], local_sem.at[KT + CT])
        fetch.start()
        fetch.wait()

    fetch_table(NEXT)

    @pl.when(odd == 1)
    def _():
        far_table.start()

    def part_own(c, carry):
        part[c] = product(WITH_OWN, 0, c)
        return carry

    early = CHUNKS - PIECES // 2
    for q in range(CHUNKS):
        if q + 1 < CHUNKS:
            send_b(q).wait_send()
            send_b(q + 1).start()
        if q == early:
            for i in (WITH_OWN, WITH_NEXT):
                fetch_table(i)
                send_a(2 * i).wait_recv()
            for i in (WITH_OWN, WITH_NEXT):
                unpack_a(i, lambda t: a_got[i, table_at[i, 0, t]])
        if q >= early:
            lax.fori_loop(2 * (q - early), 2 * (q - early) + 2, part_own, 0)
        send_b(q).wait_recv()

        @pl.when(odd == 1)
        def _():
            send_far(q).start()

        lax.fori_loop(q * PER, (q + 1) * PER, stage_b, 0)

    for c in range(PIECES):
        unpack_b(1, lambda t: b_stage[table_at[NEXT, 0, t]], c, c + 1)
        part[c] += product(WITH_NEXT, 1, c)
        for g in range(GROUPS):
            rows = slice(g * SPAN, (g + 1) * SPAN)
            values = part[c, rows, :]
            most = jnp.maximum(jnp.max(jnp.abs(values), axis=0, keepdims=True), 1e-33)
            code_out[c, rows, :] = jnp.round(values * (TOP / most)).astype(jnp.int32).astype(jnp.int16)
            scale_out[c, g : g + 1, :] = most * (1.0 / TOP)
        if c >= 3:
            send_code(c - 3).wait_send()
        send_scale(c).start()
        send_code(c).start()
        if c == 1:
            each_taker((LOCAL,), lambda copy: copy.start())

    @pl.when(odd == 1)
    def _():
        fetch_table(FAR)
        for q in range(CHUNKS):
            send_far(q).wait_recv()
        unpack_b(1, lambda t: b_got[1, table_at[FAR, 0, t]], 0, PIECES)

    fetch_table(LOCAL)
    send_a(2 * LOCAL).wait_recv()
    unpack_a(LOCAL, lambda t: a_near[table_at[LOCAL, 0, t]])

    def second_term(c, carry):
        total[c] += product(LOCAL, 1, c)
        return carry

    lax.fori_loop(0, PIECES, second_term, 0)

    def store(c):
        return pltpu.make_async_copy(result.at[c], out_ref.at[:, pl.ds(c * WIDE, WIDE)], out_sem.at[c])

    for c in range(PIECES):
        send_scale(c).wait_recv()
        send_code(c).wait_recv()
        for g in range(GROUPS):
            rows = slice(g * SPAN, (g + 1) * SPAN)
            other = code_in[c, rows, :].astype(jnp.int32).astype(jnp.float32) * scale_in[c, g : g + 1, :]
            result[c, rows, :] = (total[c, rows, :] + other).astype(jnp.bfloat16)
        store(c).start()

    each_taker((WITH_OWN, WITH_NEXT, LOCAL), lambda copy: copy.wait_send())
    next_table.wait_send()
    for q in range(CHUNKS - 1, CHUNKS):
        send_b(q).wait_send()

    @pl.when(odd == 1)
    def _():
        far_table.wait_send()
        for q in range(CHUNKS):
            send_far(q).wait_send()

    for c in range(PIECES):
        send_scale(c).wait_send()
        if c >= PIECES - 3:
            send_code(c).wait_send()
        store(c).wait()


def per_device(left_panels, right_panels, left_pattern, right_pattern):
    smem = pl.BlockSpec(memory_space=pltpu.SMEM)
    anywhere = pl.BlockSpec(memory_space=pl.ANY)
    rows, cols, inner = RT * TILE, CT * TILE, KT * TILE
    bf16, f32, dma = jnp.bfloat16, jnp.float32, pltpu.SemaphoreType.DMA
    return pl.pallas_call(
        main_kernel,
        out_shape=jax.ShapeDtypeStruct((rows, cols), bf16),
        in_specs=[anywhere, anywhere, smem, smem],
        out_specs=anywhere,
        scratch_shapes=[
            pltpu.SMEM((1, TILE), jnp.int32),
            pltpu.SMEM((1, TILE), jnp.int32),
            pltpu.SMEM((1, 2 * TILE), jnp.int32),
            pltpu.SMEM((1, 2 * TILE), jnp.int32),
            pltpu.VMEM((1, TILE), jnp.int32),
            pltpu.VMEM((1, TILE), jnp.int32),
            pltpu.VMEM((RT * KT, TILE, TILE), bf16),
            pltpu.VMEM((KT * CT, TILE, TILE), bf16),
            pltpu.VMEM((CAP + 1, TILE, TILE), bf16),
            pltpu.VMEM((CAPB + 1, TILE, TILE), bf16),
            pltpu.VMEM((2, CAP + 1, TILE, TILE), bf16),
            pltpu.VMEM((CAP + 1, TILE, TILE), bf16),
            pltpu.VMEM((2, CAPB + 1, TILE, TILE), bf16),
            pltpu.VMEM((CAPB + 1, TILE, TILE), bf16),
            pltpu.VMEM((5, 1, TILE), jnp.int32),
            pltpu.SMEM((5, 1, TILE), jnp.int32),
            pltpu.VMEM((4, rows, inner), bf16),
            pltpu.VMEM((2, PIECES, inner, WIDE), bf16),
            pltpu.VMEM((PIECES, rows, WIDE), f32),
            pltpu.VMEM((PIECES, rows, WIDE), f32),
            pltpu.VMEM((PIECES, rows, WIDE), jnp.int16),
            pltpu.VMEM((PIECES, GROUPS, WIDE), f32),
            pltpu.VMEM((PIECES, rows, WIDE), jnp.int16),
            pltpu.VMEM((PIECES, GROUPS, WIDE), f32),
            pltpu.VMEM((PIECES, rows, WIDE), bf16),
            dma((KT + CT + 1,)),
            dma((len(TAKERS) + 2,)),
            dma((5,)),
            dma((len(TAKERS),)),
            dma((3,)),
            dma((2, CHUNKS)),
            dma((2, CHUNKS)),
            dma((2, PIECES)),
            dma((2, PIECES)),
            dma((PIECES,)),
        ],
        compiler_params=pltpu.CompilerParams(
            collective_id=0, has_side_effects=True, vmem_limit_bytes=60 * 2**20
        ),
        cost_estimate=pl.CostEstimate(flops=8 * rows * inner * cols, bytes_accessed=2**23, transcendentals=0),
        name="exchange_and_multiply",
    )(left_panels.reshape(RT, TILE, inner), right_panels.reshape(KT, TILE, cols), left_pattern, right_pattern)


def solution(mesh):
    placed = (P("row", "col"), P("row", "col"), P("row", "col"), P("row", "col"))
    return jax.shard_map(
        per_device, mesh=mesh, in_specs=placed, out_specs=P("row", "col"), check_vma=False
    )
```

```python
import functools

import jax
import jax.numpy as jnp
from jax import lax
from jax.experimental import pallas as pl
from jax.experimental.pallas import tpu as pltpu
from jax.sharding import PartitionSpec as P

TILE = 128
RT, KT, CT = 4, 8, 16
CAP, CAPB = 24, 96
CHUNKS = 8
PER = CAPB // CHUNKS
WIDE = 256
PIECES = CT * TILE // WIDE
GROUPS = 8
SPAN = RT * TILE // GROUPS
TOP = 32767.0
MESH = pl.DeviceIdType.MESH
WITH_OWN, WITH_NEXT, LOCAL, NEXT, FAR = range(5)
TAKERS = (
    (WITH_OWN, 1, -1, 0), (WITH_OWN, 3, -3, 1),
    (WITH_NEXT, 1, -2, 0), (WITH_NEXT, 3, -2, 1),
    (LOCAL, 0, -1, 0), (LOCAL, 0, -3, 1),
)


def main_kernel(
    a_ref, b_ref, left_ref, right_ref, out_ref,
    a_slot, b_slot, a_after, b_after, a_table, b_table,
    a_in, b_in, a_pack, b_pack, a_got, a_near, b_got, b_stage, table_got, table_at,
    a_full, b_full, total, part, code_out, scale_out, code_in, scale_in, result,
    local_sem, table_send, table_recv, a_send, a_recv, b_send, b_recv, p_send, p_recv, out_sem,
):
    n_row, n_col = lax.axis_size("row"), lax.axis_size("col")
    row, col = lax.axis_index("row"), lax.axis_index("col")

    def at(i, j):
        return (lax.rem(row + i + n_row, n_row), lax.rem(col + j + n_col, n_col))

    def parity(i, j):
        return lax.rem(i + j, 2)

    odd = parity(row, col)
    takes = [jnp.where(parity(*at(i, j)) == want, 1, 0) for _, i, j, want in TAKERS]
    b_target, b_source = at(1 - 2 * odd, 0), at(1 - 2 * odd, 0)
    p_target, p_source = at(-1 - 2 * odd, 0), at(3 - 2 * odd, 0)
    far_target, far_source = at(-4, 0), at(4, 0)
    a_sources = (at(-1 - 2 * odd, 1 + 2 * odd), at(-1 - 2 * odd, 2), at(0, 1 + 2 * odd))

    barrier = pltpu.get_barrier_semaphore()
    for source in (*a_sources, b_source, p_source):
        pl.semaphore_signal(barrier, inc=1, device_id=source, device_id_type=MESH)

    @pl.when(odd == 1)
    def _():
        pl.semaphore_signal(barrier, inc=1, device_id=far_source, device_id_type=MESH)

    def load_a(k):
        return pltpu.make_async_copy(
            a_ref.at[:, :, pl.ds(k * TILE, TILE)], a_in.at[pl.ds(k * RT, RT)], local_sem.at[k])

    def load_b(c):
        return pltpu.make_async_copy(
            b_ref.at[:, :, pl.ds(c * TILE, TILE)], b_in.at[pl.ds(c * KT, KT)], local_sem.at[KT + c])

    for k in range(KT):
        load_a(k).start()
    for c in range(CT):
        load_b(c).start()

    blank = jnp.zeros((TILE, TILE), jnp.bfloat16)
    a_pack[CAP] = blank
    b_pack[CAPB] = blank
    for i in range(2):
        a_got[i, CAP] = blank
    a_near[CAP] = blank
    b_got[1, CAPB] = blank
    b_stage[CAPB] = blank

    def number(there, count, slot, after, blank_slot):
        def walk(t, taken):
            slot[0, t] = jnp.where(there(t) > 0, taken, blank_slot)
            return taken + jnp.where(there(t) > 0, 1, 0)

        lax.fori_loop(0, count, walk, 0)

        def back(n, found):
            t = count - 1 - n
            found = jnp.where(there(t) > 0, t, found)
            after[0, t] = found
            return found

        after[0, count] = count - 1
        lax.fori_loop(0, count, back, count - 1)

    def pack_a(n, start):
        t = a_after[0, start]
        a_pack[n] = a_in[t]
        return t + 1

    def pack_b(n, start):
        t = b_after[0, start]
        b_pack[n] = b_in[t]
        return t + 1

    def stage_b(n, carry):
        b_stage[n] = b_got[0, n]
        return carry

    def send_table(n, i, source, target):
        return pltpu.make_async_remote_copy(
            source, table_got.at[i], table_send.at[n], table_recv.at[i], device_id=target, device_id_type=MESH)

    def send_a(n):
        use, i, j, _ = TAKERS[n]
        place = a_near if use == LOCAL else a_got.at[use]
        return pltpu.make_async_remote_copy(
            a_pack.at[pl.ds(0, CAP)], place.at[pl.ds(0, CAP)], a_send.at[n], a_recv.at[use],
            device_id=at(i, j), device_id_type=MESH)

    def each_taker(uses, act):
        for n, (use, i, j, _) in enumerate(TAKERS):
            if use in uses:

                @pl.when(takes[n] == 1)
                def _():
                    act(send_table(n, use, a_table, at(i, j)))
                    act(send_a(n))

    def send_b(q):
        where = pl.ds(q * PER, PER)
        return pltpu.make_async_remote_copy(
            b_pack.at[where], b_got.at[0, where], b_send.at[0, q], b_recv.at[0, q],
            device_id=b_target, device_id_type=MESH)

    def send_far(q):
        where = pl.ds(q * PER, PER)
        return pltpu.make_async_remote_copy(
            b_got.at[0, where], b_got.at[1, where], b_send.at[1, q], b_recv.at[1, q],
            device_id=far_target, device_id_type=MESH)

    next_table = send_table(len(TAKERS), NEXT, b_table, b_target)
    far_table = send_table(len(TAKERS) + 1, FAR, table_got.at[NEXT], far_target)

    def send_code(c):
        return pltpu.make_async_remote_copy(
            code_out.at[c], code_in.at[c], p_send.at[0, c], p_recv.at[0, c], device_id=p_target, device_id_type=MESH)

    def send_scale(c):
        return pltpu.make_async_remote_copy(
            scale_out.at[c], scale_in.at[c], p_send.at[1, c], p_recv.at[1, c], device_id=p_target, device_id_type=MESH)

    def publish(slot, table):
        copy = pltpu.make_async_copy(slot, table, local_sem.at[KT + CT])
        copy.start()
        copy.wait()

    number(lambda t: left_ref[t % RT, t // RT], RT * KT, a_slot, a_after, CAP)
    publish(a_slot, a_table)
    for k in range(KT):
        load_a(k).wait()
    lax.fori_loop(0, CAP, pack_a, 0)
    pl.semaphore_wait(barrier, 2 + odd + sum(takes))
    each_taker((WITH_OWN, WITH_NEXT), lambda copy: copy.start())
    number(lambda t: right_ref[t % KT, t // KT], KT * CT, b_slot, b_after, CAPB)
    publish(b_slot, b_table)
    next_table.start()
    for c in range(CT):
        load_b(c).wait()
    lax.fori_loop(0, CAPB, pack_b, 0)
    send_b(0).start()

    def unpack_a(i, tile_of):
        for k in range(KT):
            for r in range(RT):
                a_full[i, r * TILE : (r + 1) * TILE, k * TILE : (k + 1) * TILE] = tile_of(k * RT + r)

    def unpack_b(i, tile_of, first, last):
        def one(c, carry):
            for half in range(WIDE // TILE):
                for k in range(KT):
                    tile = tile_of((c * (WIDE // TILE) + half) * KT + k)
                    b_full[i, c, k * TILE : (k + 1) * TILE, half * TILE : (half + 1) * TILE] = tile
            return carry

        lax.fori_loop(first, last, one, 0)

    def product(i, j, c):
        return jnp.dot(a_full[i], b_full[j, c], preferred_element_type=jnp.float32)

    unpack_a(3, lambda t: a_pack[a_slot[0, t]])
    unpack_b(0, lambda t: b_pack[b_slot[0, t]], 0, PIECES)

    def first_term(c, carry):
        total[c] = product(3, 0, c)
        return carry

    lax.fori_loop(0, PIECES, first_term, 0)

    def fetch_table(i):
        send_table(0, i, a_table, b_target).wait_recv()
        fetch = pltpu.make_async_copy(table_got.at[i], table_at.at[i], local_sem.at[KT + CT])
        fetch.start()
        fetch.wait()

    fetch_table(NEXT)

    @pl.when(odd == 1)
    def _():
        far_table.start()

    def part_own(c, carry):
        part[c] = product(WITH_OWN, 0, c)
        return carry

    early = CHUNKS - PIECES // 2
    for q in range(CHUNKS):
        if q + 1 < CHUNKS:
            send_b(q).wait_send()
            send_b(q + 1).start()
        if q + 1 == CHUNKS:
            each_taker((LOCAL,), lambda copy: copy.start())
        if q == early:
            for i in (WITH_OWN, WITH_NEXT):
                fetch_table(i)
                send_a(2 * i).wait_recv()
            for i in (WITH_OWN, WITH_NEXT):
                unpack_a(i, lambda t: a_got[i, table_at[i, 0, t]])
        if q >= early:
            lax.fori_loop(2 * (q - early), 2 * (q - early) + 2, part_own, 0)
        send_b(q).wait_recv()

        @pl.when(odd == 1)
        def _():
            send_far(q).start()

        lax.fori_loop(q * PER, (q + 1) * PER, stage_b, 0)

    for c in range(PIECES):
        unpack_b(1, lambda t: b_stage[table_at[NEXT, 0, t]], c, c + 1)
        part[c] += product(WITH_NEXT, 1, c)
        for g in range(GROUPS):
            rows = slice(g * SPAN, (g + 1) * SPAN)
            values = part[c, rows, :]
            most = jnp.maximum(jnp.max(jnp.abs(values), axis=0, keepdims=True), 1e-33)
            code_out[c, rows, :] = jnp.round(values * (TOP / most)).astype(jnp.int32).astype(jnp.int16)
            scale_out[c, g : g + 1, :] = most * (1.0 / TOP)
        if c >= 3:
            send_code(c - 3).wait_send()
        send_scale(c).start()
        send_code(c).start()

    @pl.when(odd == 1)
    def _():
        fetch_table(FAR)
        for q in range(CHUNKS):
            send_far(q).wait_recv()
        unpack_b(1, lambda t: b_got[1, table_at[FAR, 0, t]], 0, PIECES)

    fetch_table(LOCAL)
    send_a(2 * LOCAL).wait_recv()
    unpack_a(LOCAL, lambda t: a_near[table_at[LOCAL, 0, t]])

    def second_term(c, carry):
        total[c] += product(LOCAL, 1, c)
        return carry

    lax.fori_loop(0, PIECES, second_term, 0)

    def store(c):
        return pltpu.make_async_copy(result.at[c], out_ref.at[:, pl.ds(c * WIDE, WIDE)], out_sem.at[c])

    for c in range(PIECES):
        send_scale(c).wait_recv()
        send_code(c).wait_recv()
        for g in range(GROUPS):
            rows = slice(g * SPAN, (g + 1) * SPAN)
            other = code_in[c, rows, :].astype(jnp.int32).astype(jnp.float32) * scale_in[c, g : g + 1, :]
            result[c, rows, :] = (total[c, rows, :] + other).astype(jnp.bfloat16)
        store(c).start()

    each_taker((WITH_OWN, WITH_NEXT, LOCAL), lambda copy: copy.wait_send())
    next_table.wait_send()
    for q in range(CHUNKS - 1, CHUNKS):
        send_b(q).wait_send()

    @pl.when(odd == 1)
    def _():
        far_table.wait_send()
        for q in range(CHUNKS):
            send_far(q).wait_send()

    for c in range(PIECES):
        send_scale(c).wait_send()
        if c >= PIECES - 3:
            send_code(c).wait_send()
        store(c).wait()


def per_device(left_panels, right_panels, left_pattern, right_pattern):
    smem = pl.BlockSpec(memory_space=pltpu.SMEM)
    anywhere = pl.BlockSpec(memory_space=pl.ANY)
    rows, cols, inner = RT * TILE, CT * TILE, KT * TILE
    bf16, f32, dma = jnp.bfloat16, jnp.float32, pltpu.SemaphoreType.DMA
    return pl.pallas_call(
        main_kernel,
        out_shape=jax.ShapeDtypeStruct((rows, cols), bf16),
        in_specs=[anywhere, anywhere, smem, smem],
        out_specs=anywhere,
        scratch_shapes=[
            pltpu.SMEM((1, TILE), jnp.int32),
            pltpu.SMEM((1, TILE), jnp.int32),
            pltpu.SMEM((1, 2 * TILE), jnp.int32),
            pltpu.SMEM((1, 2 * TILE), jnp.int32),
            pltpu.VMEM((1, TILE), jnp.int32),
            pltpu.VMEM((1, TILE), jnp.int32),
            pltpu.VMEM((RT * KT, TILE, TILE), bf16),
            pltpu.VMEM((KT * CT, TILE, TILE), bf16),
            pltpu.VMEM((CAP + 1, TILE, TILE), bf16),
            pltpu.VMEM((CAPB + 1, TILE, TILE), bf16),
            pltpu.VMEM((2, CAP + 1, TILE, TILE), bf16),
            pltpu.VMEM((CAP + 1, TILE, TILE), bf16),
            pltpu.VMEM((2, CAPB + 1, TILE, TILE), bf16),
            pltpu.VMEM((CAPB + 1, TILE, TILE), bf16),
            pltpu.VMEM((5, 1, TILE), jnp.int32),
            pltpu.SMEM((5, 1, TILE), jnp.int32),
            pltpu.VMEM((4, rows, inner), bf16),
            pltpu.VMEM((2, PIECES, inner, WIDE), bf16),
            pltpu.VMEM((PIECES, rows, WIDE), f32),
            pltpu.VMEM((PIECES, rows, WIDE), f32),
            pltpu.VMEM((PIECES, rows, WIDE), jnp.int16),
            pltpu.VMEM((PIECES, GROUPS, WIDE), f32),
            pltpu.VMEM((PIECES, rows, WIDE), jnp.int16),
            pltpu.VMEM((PIECES, GROUPS, WIDE), f32),
            pltpu.VMEM((PIECES, rows, WIDE), bf16),
            dma((KT + CT + 1,)),
            dma((len(TAKERS) + 2,)),
            dma((5,)),
            dma((len(TAKERS),)),
            dma((3,)),
            dma((2, CHUNKS)),
            dma((2, CHUNKS)),
            dma((2, PIECES)),
            dma((2, PIECES)),
            dma((PIECES,)),
        ],
        compiler_params=pltpu.CompilerParams(
            collective_id=0, has_side_effects=True, vmem_limit_bytes=60 * 2**20
        ),
        cost_estimate=pl.CostEstimate(flops=8 * rows * inner * cols, bytes_accessed=2**23, transcendentals=0),
        name="exchange_and_multiply",
    )(left_panels.reshape(RT, TILE, inner), right_panels.reshape(KT, TILE, cols), left_pattern, right_pattern)


def solution(mesh):
    placed = (P("row", "col"), P("row", "col"), P("row", "col"), P("row", "col"))
    return jax.shard_map(
        per_device, mesh=mesh, in_specs=placed, out_specs=P("row", "col"), check_vma=False
    )
```

```python
import functools

import jax
import jax.numpy as jnp
from jax import lax
from jax.experimental import pallas as pl
from jax.experimental.pallas import tpu as pltpu
from jax.sharding import PartitionSpec as P

TILE = 128
RT, KT, CT = 4, 8, 16
CAP, CAPB = 24, 96
CHUNKS = 8
PER = CAPB // CHUNKS
WIDE = 256
PIECES = CT * TILE // WIDE
GROUPS = 8
SPAN = RT * TILE // GROUPS
TOP = 32767.0
MESH = pl.DeviceIdType.MESH
WITH_OWN, WITH_NEXT, LOCAL, NEXT, FAR = range(5)
TAKERS = (
    (WITH_OWN, 1, -1, 0), (WITH_OWN, 3, -3, 1),
    (WITH_NEXT, 1, -2, 0), (WITH_NEXT, 3, -2, 1),
    (LOCAL, 0, -1, 0), (LOCAL, 0, -3, 1),
)


def main_kernel(
    a_ref, b_ref, left_ref, right_ref, out_ref,
    a_slot, b_slot, a_after, b_after, a_table, b_table,
    a_in, b_in, a_pack, b_pack, a_got, a_near, b_got, b_stage, table_got, table_at,
    a_full, b_full, total, part, code_out, scale_out, code_in, scale_in, result,
    local_sem, table_send, table_recv, a_send, a_recv, b_send, b_recv, p_send, p_recv, out_sem,
):
    n_row, n_col = lax.axis_size("row"), lax.axis_size("col")
    row, col = lax.axis_index("row"), lax.axis_index("col")

    def at(i, j):
        return (lax.rem(row + i + n_row, n_row), lax.rem(col + j + n_col, n_col))

    def parity(i, j):
        return lax.rem(i + j, 2)

    odd = parity(row, col)
    takes = [jnp.where(parity(*at(i, j)) == want, 1, 0) for _, i, j, want in TAKERS]
    b_target, b_source = at(1 - 2 * odd, 0), at(1 - 2 * odd, 0)
    p_target, p_source = at(-1 - 2 * odd, 0), at(3 - 2 * odd, 0)
    far_target, far_source = at(-4, 0), at(4, 0)
    a_sources = (at(-1 - 2 * odd, 1 + 2 * odd), at(-1 - 2 * odd, 2), at(0, 1 + 2 * odd))

    barrier = pltpu.get_barrier_semaphore()
    for source in (*a_sources, b_source, p_source):
        pl.semaphore_signal(barrier, inc=1, device_id=source, device_id_type=MESH)

    @pl.when(odd == 1)
    def _():
        pl.semaphore_signal(barrier, inc=1, device_id=far_source, device_id_type=MESH)

    def load_a(k):
        return pltpu.make_async_copy(
            a_ref.at[:, :, pl.ds(k * TILE, TILE)], a_in.at[pl.ds(k * RT, RT)], local_sem.at[k])

    def load_b(c):
        return pltpu.make_async_copy(
            b_ref.at[:, :, pl.ds(c * TILE, TILE)], b_in.at[pl.ds(c * KT, KT)], local_sem.at[KT + c])

    for k in range(KT):
        load_a(k).start()
    for c in range(CT):
        load_b(c).start()

    blank = jnp.zeros((TILE, TILE), jnp.bfloat16)
    a_pack[CAP] = blank
    b_pack[CAPB] = blank
    for i in range(2):
        a_got[i, CAP] = blank
    a_near[CAP] = blank
    b_got[1, CAPB] = blank
    b_stage[CAPB] = blank

    def number(there, count, slot, after, blank_slot):
        def walk(t, taken):
            slot[0, t] = jnp.where(there(t) > 0, taken, blank_slot)
            return taken + jnp.where(there(t) > 0, 1, 0)

        lax.fori_loop(0, count, walk, 0)

        def back(n, found):
            t = count - 1 - n
            found = jnp.where(there(t) > 0, t, found)
            after[0, t] = found
            return found

        after[0, count] = count - 1
        lax.fori_loop(0, count, back, count - 1)

    def pack_a(n, start):
        t = a_after[0, start]
        a_pack[n] = a_in[t]
        return t + 1

    def pack_b(n, start):
        t = b_after[0, start]
        b_pack[n] = b_in[t]
        return t + 1

    def stage_b(n, carry):
        b_stage[n] = b_got[0, n]
        return carry

    def send_table(n, i, source, target):
        return pltpu.make_async_remote_copy(
            source, table_got.at[i], table_send.at[n], table_recv.at[i], device_id=target, device_id_type=MESH)

    def send_a(n):
        use, i, j, _ = TAKERS[n]
        place = a_near if use == LOCAL else a_got.at[use]
        return pltpu.make_async_remote_copy(
            a_pack.at[pl.ds(0, CAP)], place.at[pl.ds(0, CAP)], a_send.at[n], a_recv.at[use],
            device_id=at(i, j), device_id_type=MESH)

    def each_taker(uses, act):
        for n, (use, i, j, _) in enumerate(TAKERS):
            if use in uses:

                @pl.when(takes[n] == 1)
                def _():
                    act(send_table(n, use, a_table, at(i, j)))
                    act(send_a(n))

    def send_b(q):
        where = pl.ds(q * PER, PER)
        return pltpu.make_async_remote_copy(
            b_pack.at[where], b_got.at[0, where], b_send.at[0, q], b_recv.at[0, q],
            device_id=b_target, device_id_type=MESH)

    def send_far(q):
        where = pl.ds(q * PER, PER)
        return pltpu.make_async_remote_copy(
            b_got.at[0, where], b_got.at[1, where], b_send.at[1, q], b_recv.at[1, q],
            device_id=far_target, device_id_type=MESH)

    next_table = send_table(len(TAKERS), NEXT, b_table, b_target)
    far_table = send_table(len(TAKERS) + 1, FAR, table_got.at[NEXT], far_target)

    def send_code(c):
        return pltpu.make_async_remote_copy(
            code_out.at[c], code_in.at[c], p_send.at[0, c], p_recv.at[0, c], device_id=p_target, device_id_type=MESH)

    def send_scale(c):
        return pltpu.make_async_remote_copy(
            scale_out.at[c], scale_in.at[c], p_send.at[1, c], p_recv.at[1, c], device_id=p_target, device_id_type=MESH)

    def publish(slot, table):
        copy = pltpu.make_async_copy(slot, table, local_sem.at[KT + CT])
        copy.start()
        copy.wait()

    number(lambda t: left_ref[t % RT, t // RT], RT * KT, a_slot, a_after, CAP)
    publish(a_slot, a_table)
    for k in range(KT):
        load_a(k).wait()
    lax.fori_loop(0, CAP, pack_a, 0)
    pl.semaphore_wait(barrier, 2 + odd + sum(takes))
    each_taker((WITH_OWN, WITH_NEXT), lambda copy: copy.start())
    number(lambda t: right_ref[t % KT, t // KT], KT * CT, b_slot, b_after, CAPB)
    publish(b_slot, b_table)
    next_table.start()
    for c in range(CT):
        load_b(c).wait()
    lax.fori_loop(0, CAPB, pack_b, 0)
    send_b(0).start()

    def unpack_a(i, tile_of):
        for k in range(KT):
            for r in range(RT):
                a_full[i, r * TILE : (r + 1) * TILE, k * TILE : (k + 1) * TILE] = tile_of(k * RT + r)

    def unpack_b(i, tile_of, first, last):
        def one(c, carry):
            for half in range(WIDE // TILE):
                for k in range(KT):
                    tile = tile_of((c * (WIDE // TILE) + half) * KT + k)
                    b_full[i, c, k * TILE : (k + 1) * TILE, half * TILE : (half + 1) * TILE] = tile
            return carry

        lax.fori_loop(first, last, one, 0)

    def product(i, j, c):
        return jnp.dot(a_full[i], b_full[j, c], preferred_element_type=jnp.float32)

    unpack_a(3, lambda t: a_pack[a_slot[0, t]])
    unpack_b(0, lambda t: b_pack[b_slot[0, t]], 0, PIECES)

    def first_term(c, carry):
        total[c] = product(3, 0, c)
        return carry

    lax.fori_loop(0, PIECES, first_term, 0)

    def fetch_table(i):
        send_table(0, i, a_table, b_target).wait_recv()
        fetch = pltpu.make_async_copy(table_got.at[i], table_at.at[i], local_sem.at[KT + CT])
        fetch.start()
        fetch.wait()

    fetch_table(NEXT)

    @pl.when(odd == 1)
    def _():
        far_table.start()

    def part_own(c, carry):
        part[c] = product(WITH_OWN, 0, c)
        return carry

    early = CHUNKS - PIECES // 2
    for q in range(CHUNKS):
        if q + 1 < CHUNKS:
            send_b(q).wait_send()
            send_b(q + 1).start()
        if q + 2 == CHUNKS:
            each_taker((LOCAL,), lambda copy: copy.start())
        if q == early:
            for i in (WITH_OWN, WITH_NEXT):
                fetch_table(i)
                send_a(2 * i).wait_recv()
            for i in (WITH_OWN, WITH_NEXT):
                unpack_a(i, lambda t: a_got[i, table_at[i, 0, t]])
        if q >= early:
            lax.fori_loop(2 * (q - early), 2 * (q - early) + 2, part_own, 0)
        send_b(q).wait_recv()

        @pl.when(odd == 1)
        def _():
            send_far(q).start()

        lax.fori_loop(q * PER, (q + 1) * PER, stage_b, 0)

    for c in range(PIECES):
        unpack_b(1, lambda t: b_stage[table_at[NEXT, 0, t]], c, c + 1)
        part[c] += product(WITH_NEXT, 1, c)
        for g in range(GROUPS):
            rows = slice(g * SPAN, (g + 1) * SPAN)
            values = part[c, rows, :]
            most = jnp.maximum(jnp.max(jnp.abs(values), axis=0, keepdims=True), 1e-33)
            code_out[c, rows, :] = jnp.round(values * (TOP / most)).astype(jnp.int32).astype(jnp.int16)
            scale_out[c, g : g + 1, :] = most * (1.0 / TOP)
        if c >= 3:
            send_code(c - 3).wait_send()
        send_scale(c).start()
        send_code(c).start()

    @pl.when(odd == 1)
    def _():
        fetch_table(FAR)
        for q in range(CHUNKS):
            send_far(q).wait_recv()
        unpack_b(1, lambda t: b_got[1, table_at[FAR, 0, t]], 0, PIECES)

    fetch_table(LOCAL)
    send_a(2 * LOCAL).wait_recv()
    unpack_a(LOCAL, lambda t: a_near[table_at[LOCAL, 0, t]])

    def second_term(c, carry):
        total[c] += product(LOCAL, 1, c)
        return carry

    lax.fori_loop(0, PIECES, second_term, 0)

    def store(c):
        return pltpu.make_async_copy(result.at[c], out_ref.at[:, pl.ds(c * WIDE, WIDE)], out_sem.at[c])

    for c in range(PIECES):
        send_scale(c).wait_recv()
        send_code(c).wait_recv()
        for g in range(GROUPS):
            rows = slice(g * SPAN, (g + 1) * SPAN)
            other = code_in[c, rows, :].astype(jnp.int32).astype(jnp.float32) * scale_in[c, g : g + 1, :]
            result[c, rows, :] = (total[c, rows, :] + other).astype(jnp.bfloat16)
        store(c).start()

    each_taker((WITH_OWN, WITH_NEXT, LOCAL), lambda copy: copy.wait_send())
    next_table.wait_send()
    for q in range(CHUNKS - 1, CHUNKS):
        send_b(q).wait_send()

    @pl.when(odd == 1)
    def _():
        far_table.wait_send()
        for q in range(CHUNKS):
            send_far(q).wait_send()

    for c in range(PIECES):
        send_scale(c).wait_send()
        if c >= PIECES - 3:
            send_code(c).wait_send()
        store(c).wait()


def per_device(left_panels, right_panels, left_pattern, right_pattern):
    smem = pl.BlockSpec(memory_space=pltpu.SMEM)
    anywhere = pl.BlockSpec(memory_space=pl.ANY)
    rows, cols, inner = RT * TILE, CT * TILE, KT * TILE
    bf16, f32, dma = jnp.bfloat16, jnp.float32, pltpu.SemaphoreType.DMA
    return pl.pallas_call(
        main_kernel,
        out_shape=jax.ShapeDtypeStruct((rows, cols), bf16),
        in_specs=[anywhere, anywhere, smem, smem],
        out_specs=anywhere,
        scratch_shapes=[
            pltpu.SMEM((1, TILE), jnp.int32),
            pltpu.SMEM((1, TILE), jnp.int32),
            pltpu.SMEM((1, 2 * TILE), jnp.int32),
            pltpu.SMEM((1, 2 * TILE), jnp.int32),
            pltpu.VMEM((1, TILE), jnp.int32),
            pltpu.VMEM((1, TILE), jnp.int32),
            pltpu.VMEM((RT * KT, TILE, TILE), bf16),
            pltpu.VMEM((KT * CT, TILE, TILE), bf16),
            pltpu.VMEM((CAP + 1, TILE, TILE), bf16),
            pltpu.VMEM((CAPB + 1, TILE, TILE), bf16),
            pltpu.VMEM((2, CAP + 1, TILE, TILE), bf16),
            pltpu.VMEM((CAP + 1, TILE, TILE), bf16),
            pltpu.VMEM((2, CAPB + 1, TILE, TILE), bf16),
            pltpu.VMEM((CAPB + 1, TILE, TILE), bf16),
            pltpu.VMEM((5, 1, TILE), jnp.int32),
            pltpu.SMEM((5, 1, TILE), jnp.int32),
            pltpu.VMEM((4, rows, inner), bf16),
            pltpu.VMEM((2, PIECES, inner, WIDE), bf16),
            pltpu.VMEM((PIECES, rows, WIDE), f32),
            pltpu.VMEM((PIECES, rows, WIDE), f32),
            pltpu.VMEM((PIECES, rows, WIDE), jnp.int16),
            pltpu.VMEM((PIECES, GROUPS, WIDE), f32),
            pltpu.VMEM((PIECES, rows, WIDE), jnp.int16),
            pltpu.VMEM((PIECES, GROUPS, WIDE), f32),
            pltpu.VMEM((PIECES, rows, WIDE), bf16),
            dma((KT + CT + 1,)),
            dma((len(TAKERS) + 2,)),
            dma((5,)),
            dma((len(TAKERS),)),
            dma((3,)),
            dma((2, CHUNKS)),
            dma((2, CHUNKS)),
            dma((2, PIECES)),
            dma((2, PIECES)),
            dma((PIECES,)),
        ],
        compiler_params=pltpu.CompilerParams(
            collective_id=0, has_side_effects=True, vmem_limit_bytes=60 * 2**20
        ),
        cost_estimate=pl.CostEstimate(flops=8 * rows * inner * cols, bytes_accessed=2**23, transcendentals=0),
        name="exchange_and_multiply",
    )(left_panels.reshape(RT, TILE, inner), right_panels.reshape(KT, TILE, cols), left_pattern, right_pattern)


def solution(mesh):
    placed = (P("row", "col"), P("row", "col"), P("row", "col"), P("row", "col"))
    return jax.shard_map(
        per_device, mesh=mesh, in_specs=placed, out_specs=P("row", "col"), check_vma=False
    )
```
